32 devices in a mesh: groups: 2 (over x), chan: 8 (over z, y), tm: 2 (over core).
Axes of the slice: x: 2, y: 2, z: 4, core: 2. Of those that a mesh axis runs over, the one named last changes fastest.
Arguments:
- raw_strain: bfloat16 [2, 2560, 4096], P('tm', 'chan', 'groups'), parts along dimension 2
- fir_taps: float32 [64], replicated, may hold values from -0.75 to 0.75
- source_picks: int32 [16, 8, 2], P(('groups', 'chan')), parts along dimension 0, may hold values from -1 to 255, as said below
Outputs:
- correlation: float32 [201, 16, 4096], P(None, None, ('groups', 'chan', 'tm')), parts along dimension 2
The draws below stay inside these ranges and needn't reach their ends.
There are 2 independent parts, one for each index of `groups`. The reference program is written for one: setup_inputs(seed, part) draws one part's arguments, and reference() takes and returns one part's arrays. A program takes and returns all parts, laid end to end along the dimension named above; an argument that names none is the same for every part. Nothing has to cross between parts.
Inputs may be any that keep to these rules, and one draw needn't show every extreme that they name: source_picks[s, o, p] is a channel of sender block s, counted within the block, sent to owner block o in slot p, or -1 for an empty slot; the picks of one sender for one owner are distinct and fill slots 0 up to a count of 0 to 2; in every draw one owner block receives 2 rows from every sender block.
All inputs are finite; a program needn't handle non-finite values.
Results may differ from the reference program's by a relative error of at most 0.004.
Values may be sent and summed in bfloat16 or wider, within the bound.
A program may use at most 192 MiB of HBM per device.

```python
import math
import jax
import jax.numpy as jnp
from jax import lax

CH_DEV = 256
DEC = 10
TAPS = 64
HALF_WIN = 64
MAXLAG = 100
SLOT_CAP = 2
CHANNELS = 2048
RAW_BLOCK = 2560
SAMPLES = 512
SLOTS = 16
LAGS = 201
N_CHAN = 8
N_TM = 2


def draw_raw_strain(key, part):
    key = jax.random.fold_in(key, 5)
    key_noise, key_envelope, key_gain = jax.random.split(key, 3)
    block_len = DEC * 16
    block_total = RAW_BLOCK // block_len
    full_shape = (N_TM, block_total, block_len, CHANNELS)
    noise_field = jnp.clip(jax.random.normal(key_noise, full_shape, jnp.float32), -6.0, 6.0)
    envelope = jnp.exp(jax.random.uniform(key_envelope, (N_TM, block_total, 1, CHANNELS), jnp.float32, 0.0, math.log(10.0)))
    channel_gain = jnp.exp(jax.random.uniform(key_gain, (CHANNELS,), jnp.float32, -math.log(2.0), math.log(2.0)))
    values = noise_field * envelope * channel_gain
    return values.reshape(N_TM, RAW_BLOCK, CHANNELS).astype(jnp.bfloat16)


def draw_source_picks(key, part):
    key = jax.random.fold_in(key, 11)
    key_count, key_busy, key_rank = jax.random.split(key, 3)
    counts = jax.random.randint(key_count, (N_CHAN, N_CHAN), 0, SLOT_CAP + 1, dtype=jnp.int32)
    busiest = jax.random.randint(key_busy, (), 0, N_CHAN, dtype=jnp.int32)
    counts = jnp.where(jnp.arange(N_CHAN, dtype=jnp.int32)[None, :] == busiest, SLOT_CAP, counts)
    scores = jax.random.randint(key_rank, (N_CHAN, N_CHAN, CH_DEV), 0, 262144, dtype=jnp.int32) * CH_DEV + jnp.arange(CH_DEV, dtype=jnp.int32)
    ranked = jnp.argsort(scores, axis=-1)[:, :, :SLOT_CAP].astype(jnp.int32)
    slot_index = jnp.arange(SLOT_CAP, dtype=jnp.int32)
    return jnp.where(slot_index < counts[:, :, None], ranked, -1).astype(jnp.int32)


def scatter_about(rng, shape, scale, reach, kind=jnp.bfloat16):
    return jnp.clip(scale * jax.random.normal(rng, shape, jnp.float32), -reach, reach).astype(kind)


def setup_inputs(seed: int = 0, part: int = 0) -> dict:
    seeds = jax.random.split(jax.random.key(seed), 4)
    part_keys = jax.random.split(jax.random.fold_in(seeds[3], part), 4)
    raw_strain = draw_raw_strain(jax.random.fold_in(jax.random.fold_in(seeds[3], part), 71), part)
    fir_taps = scatter_about(seeds[1], (TAPS,), TAPS ** -0.5, 0.75, jnp.float32)
    source_picks = draw_source_picks(jax.random.fold_in(jax.random.fold_in(seeds[3], part), 71), part)
    return {"raw_strain": raw_strain, "fir_taps": fir_taps, "source_picks": source_picks}


epsilon = 1e-05

def filter_table(fir_taps):
    blocks = (TAPS + DEC - 1) // DEC
    padded = jnp.concatenate([jnp.zeros((blocks * DEC - TAPS,), fir_taps.dtype), fir_taps[::-1]])
    return padded.reshape(blocks, DEC)

def decimate(before, series, fir_taps):
    tap_table = filter_table(fir_taps)
    blocks = tap_table.shape[0]
    channel_width = series.shape[1]
    out_len = series.shape[0] // DEC
    joined = jnp.concatenate([before, series], axis=0).astype(jnp.float32).reshape(-1, DEC, channel_width)
    filtered = jnp.zeros((out_len, channel_width), jnp.float32)
    for block_index in range(blocks):
        filtered = filtered + jnp.einsum('jrc,r->jc', joined[block_index:block_index + out_len], tap_table[block_index], precision=lax.Precision.HIGHEST)
    return filtered

def normalize(decimated, padded):
    running = lax.reduce_window(padded, jnp.zeros((), padded.dtype), lax.add, (2 * HALF_WIN + 1, 1), (1, 1), 'VALID')
    return (decimated / (running / (2 * HALF_WIN + 1) + epsilon)).astype(jnp.bfloat16)

def correlate(extended, receivers):
    length = receivers.shape[0]
    lag_count = 2 * MAXLAG + 1
    slot_count = extended.shape[0]
    span = extended.shape[1]
    group_size = max([divisor for divisor in range(1, 17) if slot_count % divisor == 0])
    wide_receivers = receivers.astype(jnp.float32)
    grouped = extended.astype(jnp.float32).reshape(slot_count // group_size, group_size, span)

    def one_group(rows):
        tiled = jnp.tile(rows, (1, lag_count + 1))
        skewed = tiled[:, :lag_count * (span + 1)].reshape(group_size, lag_count, span + 1)
        windows = skewed[:, ::-1, :length]
        return jnp.einsum('glt,tc->lgc', windows, wide_receivers, precision=lax.Precision.HIGHEST)
    product = lax.map(one_group, grouped)
    return product.transpose(1, 0, 2, 3).reshape(lag_count, slot_count, -1)

def reference(raw_strain, fir_taps, source_picks):
    series = raw_strain.reshape(-1, CHANNELS)
    columns = series.reshape(series.shape[0], N_CHAN, CH_DEV).transpose(1, 0, 2)
    lead_rows = ((TAPS + DEC - 1) // DEC - 1) * DEC

    def prepare(column):
        before = jnp.zeros((lead_rows, CH_DEV), column.dtype)
        decimated = decimate(before, column, fir_taps)
        padded = jnp.pad(jnp.abs(decimated), ((HALF_WIN, HALF_WIN), (0, 0)))
        return normalize(decimated, padded)
    normed = lax.map(prepare, columns)
    widened = normed.astype(jnp.float32)
    positions = jnp.arange(CH_DEV, dtype=jnp.int32)
    lag_scale = 1.0 / math.sqrt(SAMPLES)

    def owner_correlation(owner_id):
        picked = source_picks[:, owner_id, :]
        onehot = (picked[:, :, None] == positions).astype(jnp.float32)
        source_rows = jnp.einsum('spc,stc->spt', onehot, widened, precision=lax.Precision.HIGHEST)
        source_rows = source_rows.astype(jnp.bfloat16).reshape(SLOTS, SAMPLES)
        extended = jnp.pad(source_rows, ((0, 0), (MAXLAG, MAXLAG)))
        return correlate(extended, normed[owner_id]) * lag_scale
    blocks = lax.map(owner_correlation, jnp.arange(N_CHAN, dtype=jnp.int32))
    return blocks.transpose(1, 2, 0, 3).reshape(LAGS, SLOTS, CHANNELS)
```

```python
import functools
import math

import jax
import jax.numpy as jnp
from jax import lax
from jax.experimental import pallas as pl
from jax.experimental.pallas import tpu as pltpu
from jax.sharding import PartitionSpec as P

DEC = 10
TAPS = 64
HALF_WIN = 64
MAXLAG = 100
LANES = 128
epsilon = 1e-05
MESH = pl.DeviceIdType.MESH


def split3(value):
    high = value.astype(jnp.bfloat16)
    rest = value - high.astype(jnp.float32)
    middle = rest.astype(jnp.bfloat16)
    low = (rest - middle.astype(jnp.float32)).astype(jnp.bfloat16)
    return high, middle, low


def exchange_kernel(
    n_chan, n_tm, raw_ref, taps_ref, picks_ref, normed_ref, ext_ref,
    send, recv, mags, picked, arrived, sems,
):
    n = n_chan * n_tm
    chan = lax.axis_index("chan")
    half = lax.axis_index("tm")
    me = chan * n_tm + half
    my_time = half * n_chan + chan

    def partner(step):
        other = lax.rem(me + step, n)
        return other, {"chan": other // n_tm, "tm": lax.rem(other, n_tm)}

    def source(step):
        other = lax.rem(me + n - step, n)
        return other, lax.rem(other, n_tm) * n_chan + other // n_tm

    barrier = pltpu.get_barrier_semaphore()
    for step in range(1, n):
        pl.semaphore_signal(barrier, inc=1, device_id=partner(step)[1], device_id_type=MESH)

    raw_rows = raw_ref.shape[1]
    own = raw_rows // DEC
    rows = send.shape[1]
    lead = lax.broadcasted_iota(jnp.int32, (rows, raw_rows), 0) * DEC + (DEC - 1)
    tap_index = lead - lax.broadcasted_iota(jnp.int32, (rows, raw_rows), 1)
    table = jnp.zeros((rows, raw_rows), jnp.float32)
    for tap in range(TAPS):
        table = jnp.where(tap_index == tap, taps_ref[tap], table)
    weights = jnp.concatenate(split3(table), axis=0)
    for block in range(n // 2):
        part = jnp.dot(
            weights, raw_ref[0, :, block * 2 * LANES : (block + 1) * 2 * LANES],
            preferred_element_type=jnp.float32,
        )
        part = part[:rows] + part[rows : 2 * rows] + part[2 * rows :]
        send[2 * block] = part[:, :LANES]
        send[2 * block + 1] = part[:, LANES:]

    pl.semaphore_wait(barrier, n - 1)

    def first(step):
        other, where = partner(step)
        return pltpu.make_async_remote_copy(
            src_ref=send.at[other], dst_ref=recv.at[my_time],
            send_sem=sems.at[0, step], recv_sem=sems.at[1, step],
            device_id=where, device_id_type=MESH,
        )

    def first_in(step):
        return pltpu.make_async_remote_copy(
            src_ref=send.at[0], dst_ref=recv.at[source(step)[1]],
            send_sem=sems.at[0, step], recv_sem=sems.at[1, step],
            device_id=partner(step)[1], device_id_type=MESH,
        )

    for step in range(1, n):
        first(step).start()
    recv[my_time] = send[me]

    samples = normed_ref.shape[0]
    mags[:HALF_WIN] = jnp.zeros((HALF_WIN, 3 * LANES), jnp.bfloat16)
    mags[HALF_WIN + samples :] = jnp.zeros((HALF_WIN, 3 * LANES), jnp.bfloat16)
    band_shape = (LANES, LANES + 2 * HALF_WIN)
    offset = lax.broadcasted_iota(jnp.int32, band_shape, 1) - lax.broadcasted_iota(
        jnp.int32, band_shape, 0
    )
    band = jnp.where((offset >= 0) & (offset <= 2 * HALF_WIN), 1.0, 0.0).astype(jnp.bfloat16)
    owners, slots = picks_ref.shape[1:]
    pick_rows = owners * slots
    row = lax.broadcasted_iota(jnp.int32, (pick_rows, LANES), 0)
    lane = lax.broadcasted_iota(jnp.int32, (pick_rows, LANES), 1) + half * LANES
    chosen = jnp.full((pick_rows, LANES), -1, jnp.int32)
    for owner in range(owners):
        for slot in range(slots):
            chosen = jnp.where(row == owner * slots + slot, picks_ref[0, owner, slot], chosen)
    onehot = jnp.where(chosen == lane, 1.0, 0.0).astype(jnp.bfloat16)

    for step in range(1, n):
        first_in(step).wait_recv()

    def decimated(slab):
        body = recv[slab, :own]
        if slab == 0:
            return body
        spill = recv[slab - 1, own:]
        return jnp.concatenate([body[: rows - own] + spill, body[rows - own :]], axis=0)

    for slab in range(n):
        value = jnp.concatenate(split3(jnp.abs(decimated(slab))), axis=1)
        mags[HALF_WIN + slab * own : HALF_WIN + (slab + 1) * own] = value

    per_tile = LANES // own
    for tile in range(samples // LANES):
        sums = jnp.dot(
            band, mags[tile * LANES : tile * LANES + band_shape[1]],
            preferred_element_type=jnp.float32,
        )
        running = sums[:, :LANES] + sums[:, LANES : 2 * LANES] + sums[:, 2 * LANES :]
        values = jnp.concatenate(
            [decimated(tile * per_tile + i) for i in range(per_tile)], axis=0
        )
        normed = (values / (running / (2 * HALF_WIN + 1) + epsilon)).astype(jnp.bfloat16)
        normed_ref[tile * LANES : (tile + 1) * LANES] = normed
        found = lax.dot_general(
            onehot, normed, (((1,), (1,)), ((), ())), preferred_element_type=jnp.float32
        )
        for owner in range(owners):
            picked[owner, tile * slots : (tile + 1) * slots] = found[
                owner * slots : (owner + 1) * slots
            ]

    def second(step):
        other, where = partner(step)
        return pltpu.make_async_remote_copy(
            src_ref=picked.at[other // n_tm], dst_ref=arrived.at[me],
            send_sem=sems.at[2, step], recv_sem=sems.at[3, step],
            device_id=where, device_id_type=MESH,
        )

    def second_in(step):
        return pltpu.make_async_remote_copy(
            src_ref=picked.at[0], dst_ref=arrived.at[source(step)[0]],
            send_sem=sems.at[2, step], recv_sem=sems.at[3, step],
            device_id=partner(step)[1], device_id_type=MESH,
        )

    for step in range(1, n):
        second(step).start()
    arrived[me] = picked[chan]
    ext_ref[...] = jnp.zeros_like(ext_ref)
    for step in range(1, n):
        second_in(step).wait_recv()
    for sender in range(n_chan):
        total = arrived[sender * n_tm]
        for other in range(1, n_tm):
            total = total + arrived[sender * n_tm + other]
        for tile in range(samples // LANES):
            ext_ref[
                sender * slots : (sender + 1) * slots, (tile + 1) * LANES : (tile + 2) * LANES
            ] = total[tile * slots : (tile + 1) * slots]
    for step in range(1, n):
        first(step).wait_send()
        second(step).wait_send()


def correlate_kernel(scale, ext_ref, normed_ref, out_ref):
    lags, slots, _ = out_ref.shape
    samples = normed_ref.shape[0]
    receivers = normed_ref[...]
    group = max(1, 128 // slots)
    for start in range(0, lags, group):
        stop = min(start + group, lags)
        windows = []
        for lag in range(start, stop):
            base = LANES + MAXLAG - lag
            windows.append(ext_ref[:, base : base + samples].astype(jnp.bfloat16))
        left = jnp.concatenate(windows, axis=0)
        found = jnp.dot(left, receivers, preferred_element_type=jnp.float32) * scale
        out_ref[start:stop] = found.reshape(stop - start, slots, LANES)


def per_device(n_chan, n_tm, raw_strain, fir_taps, source_picks):
    n = n_chan * n_tm
    own = raw_strain.shape[1] // DEC
    rows = own + 8
    samples = own * n
    slots = source_picks.shape[2]
    vmem = pl.BlockSpec(memory_space=pltpu.VMEM)
    smem = pl.BlockSpec(memory_space=pltpu.SMEM)
    normed, ext = pl.pallas_call(
        functools.partial(exchange_kernel, n_chan, n_tm),
        out_shape=(
            jax.ShapeDtypeStruct((samples, LANES), jnp.bfloat16),
            jax.ShapeDtypeStruct((n_chan * slots, samples + 2 * LANES), jnp.float32),
        ),
        in_specs=[vmem, smem, smem],
        out_specs=(vmem, vmem),
        scratch_shapes=[
            pltpu.VMEM((n, rows, LANES), jnp.float32),
            pltpu.VMEM((n, rows, LANES), jnp.float32),
            pltpu.VMEM((samples + 2 * HALF_WIN, 3 * LANES), jnp.bfloat16),
            pltpu.VMEM((n_chan, slots * samples // LANES, LANES), jnp.float32),
            pltpu.VMEM((n, slots * samples // LANES, LANES), jnp.float32),
            pltpu.SemaphoreType.DMA((4, n)),
        ],
        compiler_params=pltpu.CompilerParams(
            collective_id=0, has_side_effects=True, vmem_limit_bytes=40 * 2**20
        ),
    )(raw_strain, fir_taps, source_picks)
    return pl.pallas_call(
        functools.partial(correlate_kernel, 1.0 / math.sqrt(samples)),
        out_shape=jax.ShapeDtypeStruct((2 * MAXLAG + 1, n_chan * slots, LANES), jnp.float32),
        in_specs=[vmem, vmem],
        out_specs=vmem,
        compiler_params=pltpu.CompilerParams(vmem_limit_bytes=40 * 2**20),
    )(ext, normed)


def solution(mesh):
    placed = (P("tm", "chan", "groups"), P(), P(("groups", "chan"), None, None))
    return jax.shard_map(
        functools.partial(per_device, mesh.shape["chan"], mesh.shape["tm"]),
        mesh=mesh,
        in_specs=placed,
        out_specs=P(None, None, ("groups", "chan", "tm")),
        check_vma=False,
    )
```

```python
import functools
import math

import jax
import jax.numpy as jnp
from jax import lax
from jax.experimental import pallas as pl
from jax.experimental.pallas import tpu as pltpu
from jax.sharding import PartitionSpec as P

DEC = 10
TAPS = 64
HALF_WIN = 64
MAXLAG = 100
LANES = 128
epsilon = 1e-05
MESH = pl.DeviceIdType.MESH


def split3(value):
    high = value.astype(jnp.bfloat16)
    rest = value - high.astype(jnp.float32)
    middle = rest.astype(jnp.bfloat16)
    low = (rest - middle.astype(jnp.float32)).astype(jnp.bfloat16)
    return high, middle, low


def exchange_kernel(
    n_chan, n_tm, raw_hbm, taps_hbm, picks_hbm, normed_ref, ext_ref,
    raw_ref, taps_ref, picks_ref, send, recv, mags, picked, arrived, wide, loads, sems,
):
    n = n_chan * n_tm
    chan = lax.axis_index("chan")
    half = lax.axis_index("tm")
    me = chan * n_tm + half
    my_time = half * n_chan + chan
    order = sorted(range(n_chan), key=lambda d: abs(2 * d - n_chan))
    steps = [(d, g) for d in order for g in range(n_tm) if d or g]
    block_width = n_tm * LANES

    def partner(d, g):
        return lax.rem(chan + d, n_chan), lax.rem(half + g, n_tm)

    def target(d, g):
        other_chan, other_half = partner(d, g)
        return {"chan": other_chan, "tm": other_half}

    def source(d, g):
        return lax.rem(chan + n_chan - d, n_chan), lax.rem(half + n_tm - g, n_tm)

    def load(d):
        column = pl.multiple_of(lax.rem(chan + d, n_chan) * block_width, block_width)
        return pltpu.make_async_copy(
            raw_hbm.at[0, :, pl.ds(column, block_width)], raw_ref.at[d], loads.at[d]
        )

    taps_copy = pltpu.make_async_copy(taps_hbm, taps_ref, loads.at[n_chan])
    picks_copy = pltpu.make_async_copy(picks_hbm, picks_ref, loads.at[n_chan + 1])
    taps_copy.start()
    for d in order:
        load(d).start()
    picks_copy.start()
    barrier = pltpu.get_barrier_semaphore()
    for d, g in steps:
        pl.semaphore_signal(barrier, inc=1, device_id=target(d, g), device_id_type=MESH)

    def first(d, g):
        index = d * n_tm + g
        return pltpu.make_async_remote_copy(
            src_ref=send.at[d * n_tm + partner(d, g)[1]], dst_ref=recv.at[my_time],
            send_sem=sems.at[0, index], recv_sem=sems.at[1, index],
            device_id=target(d, g), device_id_type=MESH,
        )

    def first_in(d, g):
        index = d * n_tm + g
        from_chan, from_half = source(d, g)
        return pltpu.make_async_remote_copy(
            src_ref=send.at[0], dst_ref=recv.at[from_half * n_chan + from_chan],
            send_sem=sems.at[0, index], recv_sem=sems.at[1, index],
            device_id=target(d, g), device_id_type=MESH,
        )

    raw_rows = raw_ref.shape[1]
    own = raw_rows // DEC
    rows = send.shape[1]
    lead = lax.broadcasted_iota(jnp.int32, (rows, raw_rows), 0) * DEC + (DEC - 1)
    tap_index = lead - lax.broadcasted_iota(jnp.int32, (rows, raw_rows), 1)
    table = jnp.zeros((rows, raw_rows), jnp.float32)
    taps_copy.wait()
    for tap in range(TAPS):
        table = jnp.where(tap_index == tap, taps_ref[tap], table)
    weights = jnp.concatenate(split3(table), axis=0)
    for place, d in enumerate(order):
        load(d).wait()
        part = jnp.dot(weights, raw_ref[d], preferred_element_type=jnp.float32)
        part = part[:rows] + part[rows : 2 * rows] + part[2 * rows :]
        for h in range(n_tm):
            send[d * n_tm + h] = part[:, h * LANES : (h + 1) * LANES]
        if place == 0:
            pl.semaphore_wait(barrier, n - 1)
        for g in range(n_tm):
            if d or g:
                first(d, g).start()
    recv[my_time] = send[half]
    picks_copy.wait()

    samples = normed_ref.shape[0]
    mags[:HALF_WIN] = jnp.zeros((HALF_WIN, 3 * LANES), jnp.bfloat16)
    mags[HALF_WIN + samples :] = jnp.zeros((HALF_WIN, 3 * LANES), jnp.bfloat16)
    band_shape = (LANES, LANES + 2 * HALF_WIN)
    offset = lax.broadcasted_iota(jnp.int32, band_shape, 1) - lax.broadcasted_iota(
        jnp.int32, band_shape, 0
    )
    band = jnp.where((offset >= 0) & (offset <= 2 * HALF_WIN), 1.0, 0.0).astype(jnp.bfloat16)
    slots, owners = picks_ref.shape[1:]
    pick_rows = owners * slots
    row = lax.broadcasted_iota(jnp.int32, (pick_rows, LANES), 0)
    lane = lax.broadcasted_iota(jnp.int32, (pick_rows, LANES), 1) + half * LANES
    chosen = jnp.full((pick_rows, LANES), -1, jnp.int32)
    for owner in range(owners):
        for slot in range(slots):
            chosen = jnp.where(row == owner * slots + slot, picks_ref[0, slot, owner], chosen)
    onehot = jnp.where(chosen == lane, 1.0, 0.0).astype(jnp.bfloat16)

    for d, g in steps:
        first_in(d, g).wait_recv()

    def decimated(slab):
        body = recv[slab, :own]
        if slab == 0:
            return body
        spill = recv[slab - 1, own:]
        return jnp.concatenate([body[: rows - own] + spill, body[rows - own :]], axis=0)

    for slab in range(n):
        value = jnp.concatenate(split3(jnp.abs(decimated(slab))), axis=1)
        mags[HALF_WIN + slab * own : HALF_WIN + (slab + 1) * own] = value

    per_tile = LANES // own
    for tile in range(samples // LANES):
        sums = jnp.dot(
            band, mags[tile * LANES : tile * LANES + band_shape[1]],
            preferred_element_type=jnp.float32,
        )
        running = sums[:, :LANES] + sums[:, LANES : 2 * LANES] + sums[:, 2 * LANES :]
        values = jnp.concatenate(
            [decimated(tile * per_tile + i) for i in range(per_tile)], axis=0
        )
        normed = (values / (running / (2 * HALF_WIN + 1) + epsilon)).astype(jnp.bfloat16)
        normed_ref[tile * LANES : (tile + 1) * LANES] = normed
        found = lax.dot_general(
            onehot, normed, (((1,), (1,)), ((), ())), preferred_element_type=jnp.float32
        )
        for owner in range(owners):
            picked[owner, tile * slots : (tile + 1) * slots] = found[
                owner * slots : (owner + 1) * slots
            ]

    def second(d, g):
        index = d * n_tm + g
        return pltpu.make_async_remote_copy(
            src_ref=picked.at[partner(d, g)[0]], dst_ref=arrived.at[me],
            send_sem=sems.at[2, index], recv_sem=sems.at[3, index],
            device_id=target(d, g), device_id_type=MESH,
        )

    def second_in(d, g):
        index = d * n_tm + g
        from_chan, from_half = source(d, g)
        return pltpu.make_async_remote_copy(
            src_ref=picked.at[0], dst_ref=arrived.at[from_chan * n_tm + from_half],
            send_sem=sems.at[2, index], recv_sem=sems.at[3, index],
            device_id=target(d, g), device_id_type=MESH,
        )

    for d, g in steps:
        second(d, g).start()
    arrived[me] = picked[chan]
    edge = jnp.zeros((ext_ref.shape[0], LANES), ext_ref.dtype)
    ext_ref[:, :LANES] = edge
    ext_ref[:, LANES + samples :] = edge
    for d, g in steps:
        second_in(d, g).wait_recv()
    for sender in range(n_chan):
        total = arrived[sender * n_tm]
        for other in range(1, n_tm):
            total = total + arrived[sender * n_tm + other]
        for tile in range(samples // LANES):
            wide[
                sender * slots : (sender + 1) * slots, tile * LANES : (tile + 1) * LANES
            ] = total[tile * slots : (tile + 1) * slots]
    ext_ref[:, LANES : LANES + samples] = wide[...].astype(ext_ref.dtype)
    for d, g in steps:
        first(d, g).wait_send()
        second(d, g).wait_send()


def correlate_kernel(scale, ext_ref, normed_ref, out_hbm, out_ref, sems):
    lags, slots, _ = out_ref.shape
    samples = normed_ref.shape[0]
    receivers = normed_ref[...]
    group = max(1, 128 // slots)
    pieces = sems.shape[0]
    piece = group * -(-lags // (group * pieces))
    copies = []
    for start in range(0, lags, group):
        stop = min(start + group, lags)
        windows = []
        for lag in range(start, stop):
            base = LANES + MAXLAG - lag
            windows.append(ext_ref[:, base : base + samples])
        left = jnp.concatenate(windows, axis=0)
        found = jnp.dot(left, receivers, preferred_element_type=jnp.float32) * scale
        out_ref[start:stop] = found.reshape(stop - start, slots, LANES)
        if stop % piece == 0 or stop == lags:
            begin = len(copies) * piece
            copy = pltpu.make_async_copy(
                out_ref.at[begin:stop], out_hbm.at[begin:stop], sems.at[len(copies)]
            )
            copy.start()
            copies.append(copy)
    for copy in copies:
        copy.wait()


def per_device(n_chan, n_tm, raw_strain, fir_taps, source_picks):
    n = n_chan * n_tm
    own = raw_strain.shape[1] // DEC
    rows = own + 8
    samples = own * n
    slots = source_picks.shape[2]
    vmem = pl.BlockSpec(memory_space=pltpu.VMEM)
    anywhere = pl.BlockSpec(memory_space=pl.ANY)
    picks = source_picks.transpose(0, 2, 1)
    traces = n_chan * slots
    normed, ext = pl.pallas_call(
        functools.partial(exchange_kernel, n_chan, n_tm),
        out_shape=(
            jax.ShapeDtypeStruct((samples, LANES), jnp.bfloat16),
            jax.ShapeDtypeStruct((traces, samples + 2 * LANES), jnp.bfloat16),
        ),
        in_specs=[anywhere, anywhere, anywhere],
        out_specs=(vmem, vmem),
        scratch_shapes=[
            pltpu.VMEM((n_chan, raw_strain.shape[1], n_tm * LANES), jnp.bfloat16),
            pltpu.SMEM(fir_taps.shape, jnp.float32),
            pltpu.SMEM(picks.shape, jnp.int32),
            pltpu.VMEM((n, rows, LANES), jnp.float32),
            pltpu.VMEM((n, rows, LANES), jnp.float32),
            pltpu.VMEM((samples + 2 * HALF_WIN, 3 * LANES), jnp.bfloat16),
            pltpu.VMEM((n_chan, slots * samples // LANES, LANES), jnp.float32),
            pltpu.VMEM((n, slots * samples // LANES, LANES), jnp.float32),
            pltpu.VMEM((traces, samples), jnp.float32),
            pltpu.SemaphoreType.DMA((n_chan + 2,)),
            pltpu.SemaphoreType.DMA((4, n)),
        ],
        compiler_params=pltpu.CompilerParams(
            collective_id=0, has_side_effects=True, vmem_limit_bytes=60 * 2**20
        ),
    )(raw_strain, fir_taps, picks)
    out_shape = (2 * MAXLAG + 1, traces, LANES)
    return pl.pallas_call(
        functools.partial(correlate_kernel, 1.0 / math.sqrt(samples)),
        out_shape=jax.ShapeDtypeStruct(out_shape, jnp.float32),
        in_specs=[vmem, vmem],
        out_specs=anywhere,
        scratch_shapes=[
            pltpu.VMEM(out_shape, jnp.float32),
            pltpu.SemaphoreType.DMA((6,)),
        ],
        compiler_params=pltpu.CompilerParams(vmem_limit_bytes=40 * 2**20),
    )(ext, normed)


def solution(mesh):
    placed = (P("tm", "chan", "groups"), P(), P(("groups", "chan"), None, None))
    return jax.shard_map(
        functools.partial(per_device, mesh.shape["chan"], mesh.shape["tm"]),
        mesh=mesh,
        in_specs=placed,
        out_specs=P(None, None, ("groups", "chan", "tm")),
        check_vma=False,
    )
```

```python
import functools
import math

import jax
import jax.numpy as jnp
from jax import lax
from jax.experimental import pallas as pl
from jax.experimental.pallas import tpu as pltpu
from jax.sharding import PartitionSpec as P

DEC = 10
TAPS = 64
HALF_WIN = 64
MAXLAG = 100
LANES = 128
epsilon = 1e-05
MESH = pl.DeviceIdType.MESH


def split3(value):
    high = value.astype(jnp.bfloat16)
    rest = value - high.astype(jnp.float32)
    middle = rest.astype(jnp.bfloat16)
    low = (rest - middle.astype(jnp.float32)).astype(jnp.bfloat16)
    return high, middle, low


def exchange_kernel(
    n_chan, n_tm, raw_hbm, taps_hbm, picks_hbm, normed_ref, ext_ref,
    raw_ref, taps_ref, picks_ref, send, recv, mags, parts, mine, votes,
    picked, arrived, loads, sems,
):
    n = n_chan * n_tm
    chan = lax.axis_index("chan")
    half = lax.axis_index("tm")
    me = chan * n_tm + half
    my_time = half * n_chan + chan
    order = sorted(range(n_chan), key=lambda d: abs(2 * d - n_chan))
    steps = [(d, g) for d in order for g in range(n_tm) if d or g]
    block_width = n_tm * LANES

    def partner(d, g):
        return lax.rem(chan + d, n_chan), lax.rem(half + g, n_tm)

    def target(d, g):
        other_chan, other_half = partner(d, g)
        return {"chan": other_chan, "tm": other_half}

    def source(d, g):
        return lax.rem(chan + n_chan - d, n_chan), lax.rem(half + n_tm - g, n_tm)

    def load(d):
        column = pl.multiple_of(lax.rem(chan + d, n_chan) * block_width, block_width)
        return pltpu.make_async_copy(
            raw_hbm.at[0, :, pl.ds(column, block_width)], raw_ref.at[d], loads.at[d]
        )

    taps_copy = pltpu.make_async_copy(taps_hbm, taps_ref, loads.at[n_chan])
    picks_copy = pltpu.make_async_copy(picks_hbm, picks_ref, loads.at[n_chan + 1])
    taps_copy.start()
    picks_copy.start()
    for d in order:
        load(d).start()
    barrier = pltpu.get_barrier_semaphore()
    for d, g in steps:
        pl.semaphore_signal(barrier, inc=1, device_id=target(d, g), device_id_type=MESH)

    def first(d, g):
        index = d * n_tm + g
        return pltpu.make_async_remote_copy(
            src_ref=send.at[d * n_tm + partner(d, g)[1]], dst_ref=recv.at[my_time],
            send_sem=sems.at[0, index], recv_sem=sems.at[1, index],
            device_id=target(d, g), device_id_type=MESH,
        )

    def first_in(d, g):
        index = d * n_tm + g
        from_chan, from_half = source(d, g)
        return pltpu.make_async_remote_copy(
            src_ref=send.at[0], dst_ref=recv.at[from_half * n_chan + from_chan],
            send_sem=sems.at[0, index], recv_sem=sems.at[1, index],
            device_id=target(d, g), device_id_type=MESH,
        )

    raw_rows = raw_ref.shape[1]
    own = raw_rows // DEC
    rows = send.shape[1]
    lead = lax.broadcasted_iota(jnp.int32, (rows, raw_rows), 0) * DEC + (DEC - 1)
    tap_index = lead - lax.broadcasted_iota(jnp.int32, (rows, raw_rows), 1)
    table = jnp.zeros((rows, raw_rows), jnp.float32)
    taps_copy.wait()
    for tap in range(TAPS):
        table = jnp.where(tap_index == tap, taps_ref[tap], table)
    weights = jnp.concatenate(split3(table), axis=0)
    slots, owners = picks_ref.shape[1:]
    traces = n_chan * slots
    picks_copy.wait()
    lane = lax.broadcasted_iota(jnp.int32, mine.shape, 1)
    vote = jnp.full(mine.shape, -1, jnp.int32)
    for owner in range(owners):
        for slot in range(slots):
            spot = owner * traces + chan * slots + slot
            vote = jnp.where(lane == spot, picks_ref[0, slot, owner], vote)
    mine[...] = vote.astype(jnp.float32)
    votes[0] = mine[...]

    def announce(d):
        return pltpu.make_async_remote_copy(
            src_ref=mine, dst_ref=votes.at[d],
            send_sem=sems.at[4, d], recv_sem=sems.at[5, d],
            device_id=target(n_chan - d, 0), device_id_type=MESH,
        )

    for place, d in enumerate(order):
        load(d).wait()
        part = jnp.dot(weights, raw_ref[d], preferred_element_type=jnp.float32)
        part = part[:rows] + part[rows : 2 * rows] + part[2 * rows :]
        parts[d] = jnp.concatenate(split3(part), axis=0)
        for h in range(n_tm):
            send[d * n_tm + h] = part[:, h * LANES : (h + 1) * LANES]
        if place == 0:
            pl.semaphore_wait(barrier, n - 1)
            for other in range(1, n_chan):
                announce(other).start()
        for g in range(n_tm):
            if d or g:
                first(d, g).start()
    recv[my_time] = send[half]

    samples = normed_ref.shape[0]
    width = mags.shape[1]
    mags[:HALF_WIN] = jnp.zeros((HALF_WIN, width), jnp.bfloat16)
    mags[HALF_WIN + samples :] = jnp.zeros((HALF_WIN, width), jnp.bfloat16)
    mags[HALF_WIN : HALF_WIN + samples, 3 * LANES :] = jnp.zeros(
        (samples, width - 3 * LANES), jnp.bfloat16
    )
    picked[...] = jnp.zeros_like(picked)
    edge = jnp.zeros((traces, LANES), ext_ref.dtype)
    ext_ref[:, :LANES] = edge
    ext_ref[:, LANES + samples :] = edge

    def second(d, g):
        index = d * n_tm + g
        return pltpu.make_async_remote_copy(
            src_ref=picked.at[partner(d, g)[0]], dst_ref=arrived.at[my_time],
            send_sem=sems.at[2, index], recv_sem=sems.at[3, index],
            device_id=target(d, g), device_id_type=MESH,
        )

    def second_in(d, g):
        index = d * n_tm + g
        from_chan, from_half = source(d, g)
        return pltpu.make_async_remote_copy(
            src_ref=picked.at[0], dst_ref=arrived.at[from_half * n_chan + from_chan],
            send_sem=sems.at[2, index], recv_sem=sems.at[3, index],
            device_id=target(d, g), device_id_type=MESH,
        )

    for d in range(1, n_chan):
        announce(d).wait_recv()
    columns = mine.shape[1]
    position = lax.broadcasted_iota(jnp.int32, (block_width, columns), 0).astype(jnp.float32)
    found = jnp.zeros((3 * rows, columns), jnp.float32)
    for d in range(n_chan):
        onehot = jnp.where(position == votes[d, :1], 1.0, 0.0).astype(jnp.bfloat16)
        found = found + jnp.dot(parts[d], onehot, preferred_element_type=jnp.float32)
    found = found[:rows] + found[rows : 2 * rows] + found[2 * rows :]
    for owner in range(owners):
        for piece in range(rows // 8):
            picked[owner, :, piece * traces : (piece + 1) * traces] = found[
                piece * 8 : (piece + 1) * 8, owner * traces : (owner + 1) * traces
            ]
    for d, g in steps:
        second(d, g).start()
    arrived[my_time] = picked[chan]

    band_shape = (LANES, LANES + 2 * HALF_WIN)
    offset = lax.broadcasted_iota(jnp.int32, band_shape, 1) - lax.broadcasted_iota(
        jnp.int32, band_shape, 0
    )
    band = jnp.where((offset >= 0) & (offset <= 2 * HALF_WIN), 1.0, 0.0).astype(jnp.bfloat16)
    same = lax.broadcasted_iota(jnp.int32, (traces, traces), 0) == lax.broadcasted_iota(
        jnp.int32, (traces, traces), 1
    )
    identity = jnp.where(same, 1.0, 0.0).astype(jnp.bfloat16)

    for d, g in steps:
        first_in(d, g).wait_recv()

    def decimated(slab):
        body = recv[slab, :own]
        if slab == 0:
            return body
        spill = recv[slab - 1, own:]
        return jnp.concatenate([body[: rows - own] + spill, body[rows - own :]], axis=0)

    def source_rows(slab):
        pieces = [
            arrived[slab, :, piece * traces : (piece + 1) * traces] for piece in range(own // 8)
        ]
        if slab:
            last = (own // 8) * traces
            pieces[0] = pieces[0] + arrived[slab - 1, :, last : last + traces]
        return jnp.concatenate(pieces, axis=0)

    for slab in range(n):
        value = jnp.concatenate(split3(jnp.abs(decimated(slab))), axis=1)
        mags[HALF_WIN + slab * own : HALF_WIN + (slab + 1) * own, : 3 * LANES] = value
    for d, g in steps:
        second_in(d, g).wait_recv()
    for slab in range(n):
        value = jnp.concatenate(split3(jnp.abs(source_rows(slab))), axis=1)
        mags[
            HALF_WIN + slab * own : HALF_WIN + (slab + 1) * own,
            3 * LANES : 3 * LANES + 3 * traces,
        ] = value

    def normalized(values, sums):
        wide = values.shape[1]
        running = sums[:, :wide] + sums[:, wide : 2 * wide] + sums[:, 2 * wide : 3 * wide]
        return (values / (running / (2 * HALF_WIN + 1) + epsilon)).astype(jnp.bfloat16)

    per_tile = LANES // own
    for tile in range(samples // LANES):
        sums = jnp.dot(
            band, mags[tile * LANES : tile * LANES + band_shape[1]],
            preferred_element_type=jnp.float32,
        )
        slabs = range(tile * per_tile, (tile + 1) * per_tile)
        normed_ref[tile * LANES : (tile + 1) * LANES] = normalized(
            jnp.concatenate([decimated(slab) for slab in slabs], axis=0), sums[:, : 3 * LANES]
        )
        picks = normalized(
            jnp.concatenate([source_rows(slab) for slab in slabs], axis=0), sums[:, 3 * LANES :]
        )
        turned = lax.dot_general(
            identity, picks, (((1,), (1,)), ((), ())), preferred_element_type=jnp.float32
        )
        ext_ref[:, (tile + 1) * LANES : (tile + 2) * LANES] = turned.astype(ext_ref.dtype)
    for d in range(1, n_chan):
        announce(d).wait_send()
    for d, g in steps:
        first(d, g).wait_send()
        second(d, g).wait_send()


def correlate_kernel(scale, ext_ref, normed_ref, out_hbm, out_ref, sems):
    lags, slots, _ = out_ref.shape
    samples = normed_ref.shape[0]
    receivers = normed_ref[...]
    group = max(1, 128 // slots)
    pieces = sems.shape[0]
    piece = group * -(-lags // (group * pieces))
    copies = []
    for start in range(0, lags, group):
        stop = min(start + group, lags)
        windows = []
        for lag in range(start, stop):
            base = LANES + MAXLAG - lag
            windows.append(ext_ref[:, base : base + samples])
        left = jnp.concatenate(windows, axis=0)
        found = jnp.dot(left, receivers, preferred_element_type=jnp.float32) * scale
        out_ref[start:stop] = found.reshape(stop - start, slots, LANES)
        if stop % piece == 0 or stop == lags:
            begin = len(copies) * piece
            copy = pltpu.make_async_copy(
                out_ref.at[begin:stop], out_hbm.at[begin:stop], sems.at[len(copies)]
            )
            copy.start()
            copies.append(copy)
    for copy in copies:
        copy.wait()


def per_device(n_chan, n_tm, raw_strain, fir_taps, source_picks):
    n = n_chan * n_tm
    own = raw_strain.shape[1] // DEC
    rows = own + 8
    samples = own * n
    slots = source_picks.shape[2]
    vmem = pl.BlockSpec(memory_space=pltpu.VMEM)
    anywhere = pl.BlockSpec(memory_space=pl.ANY)
    picks = source_picks.transpose(0, 2, 1)
    traces = n_chan * slots
    sum_width = 3 * LANES + pl.cdiv(3 * traces, LANES) * LANES
    tile_width = pl.cdiv(rows // 8 * traces, LANES) * LANES
    normed, ext = pl.pallas_call(
        functools.partial(exchange_kernel, n_chan, n_tm),
        out_shape=(
            jax.ShapeDtypeStruct((samples, LANES), jnp.bfloat16),
            jax.ShapeDtypeStruct((traces, samples + 2 * LANES), jnp.bfloat16),
        ),
        in_specs=[anywhere, anywhere, anywhere],
        out_specs=(vmem, vmem),
        scratch_shapes=[
            pltpu.VMEM((n_chan, raw_strain.shape[1], n_tm * LANES), jnp.bfloat16),
            pltpu.SMEM(fir_taps.shape, jnp.float32),
            pltpu.SMEM(picks.shape, jnp.int32),
            pltpu.VMEM((n, rows, LANES), jnp.float32),
            pltpu.VMEM((n, rows, LANES), jnp.float32),
            pltpu.VMEM((samples + 2 * HALF_WIN, sum_width), jnp.bfloat16),
            pltpu.VMEM((n_chan, 3 * rows, n_tm * LANES), jnp.bfloat16),
            pltpu.VMEM((8, n_chan * traces), jnp.float32),
            pltpu.VMEM((n_chan, 8, n_chan * traces), jnp.float32),
            pltpu.VMEM((n_chan, 8, tile_width), jnp.float32),
            pltpu.VMEM((n, 8, tile_width), jnp.float32),
            pltpu.SemaphoreType.DMA((n_chan + 2,)),
            pltpu.SemaphoreType.DMA((6, n)),
        ],
        compiler_params=pltpu.CompilerParams(
            collective_id=0, has_side_effects=True, vmem_limit_bytes=60 * 2**20
        ),
    )(raw_strain, fir_taps, picks)
    out_shape = (2 * MAXLAG + 1, traces, LANES)
    return pl.pallas_call(
        functools.partial(correlate_kernel, 1.0 / math.sqrt(samples)),
        out_shape=jax.ShapeDtypeStruct(out_shape, jnp.float32),
        in_specs=[vmem, vmem],
        out_specs=anywhere,
        scratch_shapes=[
            pltpu.VMEM(out_shape, jnp.float32),
            pltpu.SemaphoreType.DMA((6,)),
        ],
        compiler_params=pltpu.CompilerParams(vmem_limit_bytes=40 * 2**20),
    )(ext, normed)


def solution(mesh):
    placed = (P("tm", "chan", "groups"), P(), P(("groups", "chan"), None, None))
    return jax.shard_map(
        functools.partial(per_device, mesh.shape["chan"], mesh.shape["tm"]),
        mesh=mesh,
        in_specs=placed,
        out_specs=P(None, None, ("groups", "chan", "tm")),
        check_vma=False,
    )
```

```python
import functools
import math

import jax
import jax.numpy as jnp
from jax import lax
from jax.experimental import pallas as pl
from jax.experimental.pallas import tpu as pltpu
from jax.sharding import PartitionSpec as P

DEC = 10
TAPS = 64
HALF_WIN = 64
MAXLAG = 100
LANES = 128
epsilon = 1e-05
MESH = pl.DeviceIdType.MESH


def split3(value):
    high = value.astype(jnp.bfloat16)
    rest = value - high.astype(jnp.float32)
    middle = rest.astype(jnp.bfloat16)
    low = (rest - middle.astype(jnp.float32)).astype(jnp.bfloat16)
    return high, middle, low


def exchange_kernel(
    n_chan, n_tm, raw_hbm, taps_hbm, picks_hbm, normed_ref, ext_ref,
    raw_ref, taps_ref, picks_ref, send, recv, mags, parts, mine, votes,
    picked, arrived, loads, sems,
):
    n = n_chan * n_tm
    chan = lax.axis_index("chan")
    half = lax.axis_index("tm")
    me = chan * n_tm + half
    my_time = half * n_chan + chan
    order = sorted(range(n_chan), key=lambda d: abs(2 * d - n_chan))
    steps = [(d, g) for d in order for g in range(n_tm) if d or g]
    block_width = n_tm * LANES

    def partner(d, g):
        return lax.rem(chan + d, n_chan), lax.rem(half + g, n_tm)

    def target(d, g):
        other_chan, other_half = partner(d, g)
        return {"chan": other_chan, "tm": other_half}

    def source(d, g):
        return lax.rem(chan + n_chan - d, n_chan), lax.rem(half + n_tm - g, n_tm)

    def load(d):
        column = pl.multiple_of(lax.rem(chan + d, n_chan) * block_width, block_width)
        return pltpu.make_async_copy(
            raw_hbm.at[0, :, pl.ds(column, block_width)], raw_ref.at[d], loads.at[d]
        )

    taps_copy = pltpu.make_async_copy(taps_hbm, taps_ref, loads.at[n_chan])
    picks_copy = pltpu.make_async_copy(picks_hbm, picks_ref, loads.at[n_chan + 1])
    taps_copy.start()
    picks_copy.start()
    for d in order:
        load(d).start()
    barrier = pltpu.get_barrier_semaphore()
    for d, g in steps:
        pl.semaphore_signal(barrier, inc=1, device_id=target(d, g), device_id_type=MESH)

    def first(d, g):
        index = d * n_tm + g
        return pltpu.make_async_remote_copy(
            src_ref=send.at[d * n_tm + partner(d, g)[1]], dst_ref=recv.at[my_time],
            send_sem=sems.at[0, index], recv_sem=sems.at[1, index],
            device_id=target(d, g), device_id_type=MESH,
        )

    def first_in(d, g):
        index = d * n_tm + g
        from_chan, from_half = source(d, g)
        return pltpu.make_async_remote_copy(
            src_ref=send.at[0], dst_ref=recv.at[from_half * n_chan + from_chan],
            send_sem=sems.at[0, index], recv_sem=sems.at[1, index],
            device_id=target(d, g), device_id_type=MESH,
        )

    raw_rows = raw_ref.shape[1]
    own = raw_rows // DEC
    rows = send.shape[1]
    lead = lax.broadcasted_iota(jnp.int32, (rows, raw_rows), 0) * DEC + (DEC - 1)
    tap_index = lead - lax.broadcasted_iota(jnp.int32, (rows, raw_rows), 1)
    table = jnp.zeros((rows, raw_rows), jnp.float32)
    taps_copy.wait()
    for tap in range(TAPS):
        table = jnp.where(tap_index == tap, taps_ref[tap], table)
    weights = jnp.concatenate(split3(table), axis=0)
    slots, owners = picks_ref.shape[1:]
    traces = n_chan * slots
    picks_copy.wait()
    lane = lax.broadcasted_iota(jnp.int32, mine.shape, 1)
    vote = jnp.full(mine.shape, -1, jnp.int32)
    for owner in range(owners):
        for slot in range(slots):
            spot = owner * traces + chan * slots + slot
            vote = jnp.where(lane == spot, picks_ref[0, slot, owner], vote)
    mine[...] = vote.astype(jnp.float32)
    votes[0] = mine[...]

    def announce(d):
        return pltpu.make_async_remote_copy(
            src_ref=mine, dst_ref=votes.at[d],
            send_sem=sems.at[4, d], recv_sem=sems.at[5, d],
            device_id=target(n_chan - d, 0), device_id_type=MESH,
        )

    for place, d in enumerate(order):
        load(d).wait()
        part = jnp.dot(weights, raw_ref[d], preferred_element_type=jnp.float32)
        part = part[:rows] + part[rows : 2 * rows] + part[2 * rows :]
        parts[d] = jnp.concatenate(split3(part), axis=0)
        for h in range(n_tm):
            send[d * n_tm + h] = part[:, h * LANES : (h + 1) * LANES]
        if place == 0:
            pl.semaphore_wait(barrier, n - 1)
            for other in range(1, n_chan):
                announce(other).start()
        for g in range(n_tm):
            if d or g:
                first(d, g).start()
    recv[my_time] = send[half]

    samples = normed_ref.shape[0]
    width = mags.shape[1]
    mags[:HALF_WIN] = jnp.zeros((HALF_WIN, width), jnp.bfloat16)
    mags[HALF_WIN + samples :] = jnp.zeros((HALF_WIN, width), jnp.bfloat16)
    mags[HALF_WIN : HALF_WIN + samples, 3 * LANES :] = jnp.zeros(
        (samples, width - 3 * LANES), jnp.bfloat16
    )
    picked[...] = jnp.zeros_like(picked)
    edge = jnp.zeros((traces, LANES), ext_ref.dtype)
    ext_ref[:, :LANES] = edge
    ext_ref[:, LANES + samples :] = edge

    def second(d, g):
        index = d * n_tm + g
        return pltpu.make_async_remote_copy(
            src_ref=picked.at[partner(d, g)[0]], dst_ref=arrived.at[my_time],
            send_sem=sems.at[2, index], recv_sem=sems.at[3, index],
            device_id=target(d, g), device_id_type=MESH,
        )

    def second_in(d, g):
        index = d * n_tm + g
        from_chan, from_half = source(d, g)
        return pltpu.make_async_remote_copy(
            src_ref=picked.at[0], dst_ref=arrived.at[from_half * n_chan + from_chan],
            send_sem=sems.at[2, index], recv_sem=sems.at[3, index],
            device_id=target(d, g), device_id_type=MESH,
        )

    for d in range(1, n_chan):
        announce(d).wait_recv()
    columns = mine.shape[1]
    position = lax.broadcasted_iota(jnp.int32, (block_width, columns), 0).astype(jnp.float32)
    found = jnp.zeros((3 * rows, columns), jnp.float32)
    for d in range(n_chan):
        onehot = jnp.where(position == votes[d, :1], 1.0, 0.0).astype(jnp.bfloat16)
        found = found + jnp.dot(parts[d], onehot, preferred_element_type=jnp.float32)
    found = found[:rows] + found[rows : 2 * rows] + found[2 * rows :]
    for owner in range(owners):
        for piece in range(rows // 8):
            picked[owner, :, piece * traces : (piece + 1) * traces] = found[
                piece * 8 : (piece + 1) * 8, owner * traces : (owner + 1) * traces
            ]
    for d, g in steps:
        second(d, g).start()
    arrived[my_time] = picked[chan]

    band_shape = (LANES, LANES + 2 * HALF_WIN)
    offset = lax.broadcasted_iota(jnp.int32, band_shape, 1) - lax.broadcasted_iota(
        jnp.int32, band_shape, 0
    )
    band = jnp.where((offset >= 0) & (offset <= 2 * HALF_WIN), 1.0, 0.0).astype(jnp.bfloat16)
    same = lax.broadcasted_iota(jnp.int32, (traces, traces), 0) == lax.broadcasted_iota(
        jnp.int32, (traces, traces), 1
    )
    identity = jnp.where(same, 1.0, 0.0).astype(jnp.bfloat16)

    for d, g in steps:
        first_in(d, g).wait_recv()

    def decimated(slab):
        body = recv[slab, :own]
        if slab == 0:
            return body
        spill = recv[slab - 1, own:]
        return jnp.concatenate([body[: rows - own] + spill, body[rows - own :]], axis=0)

    def source_rows(slab):
        pieces = [
            arrived[slab, :, piece * traces : (piece + 1) * traces] for piece in range(own // 8)
        ]
        if slab:
            last = (own // 8) * traces
            pieces[0] = pieces[0] + arrived[slab - 1, :, last : last + traces]
        return jnp.concatenate(pieces, axis=0)

    for slab in range(n):
        value = jnp.concatenate(split3(jnp.abs(decimated(slab))), axis=1)
        mags[HALF_WIN + slab * own : HALF_WIN + (slab + 1) * own, : 3 * LANES] = value
    for d, g in steps:
        second_in(d, g).wait_recv()
    for slab in range(n):
        value = jnp.concatenate(split3(jnp.abs(source_rows(slab))), axis=1)
        mags[
            HALF_WIN + slab * own : HALF_WIN + (slab + 1) * own,
            3 * LANES : 3 * LANES + 3 * traces,
        ] = value

    def normalized(values, sums):
        wide = values.shape[1]
        running = sums[:, :wide] + sums[:, wide : 2 * wide] + sums[:, 2 * wide : 3 * wide]
        return (values / (running / (2 * HALF_WIN + 1) + epsilon)).astype(jnp.bfloat16)

    per_tile = LANES // own
    for tile in range(samples // LANES):
        sums = jnp.dot(
            band, mags[tile * LANES : tile * LANES + band_shape[1]],
            preferred_element_type=jnp.float32,
        )
        slabs = range(tile * per_tile, (tile + 1) * per_tile)
        normed_ref[tile * LANES : (tile + 1) * LANES] = normalized(
            jnp.concatenate([decimated(slab) for slab in slabs], axis=0), sums[:, : 3 * LANES]
        )
        picks = normalized(
            jnp.concatenate([source_rows(slab) for slab in slabs], axis=0), sums[:, 3 * LANES :]
        )
        turned = lax.dot_general(
            identity, picks, (((1,), (1,)), ((), ())), preferred_element_type=jnp.float32
        )
        ext_ref[:, (tile + 1) * LANES : (tile + 2) * LANES] = turned.astype(ext_ref.dtype)
    for d in range(1, n_chan):
        announce(d).wait_send()
    for d, g in steps:
        first(d, g).wait_send()
        second(d, g).wait_send()


def correlate_kernel(scale, ext_hbm, normed_hbm, out_hbm, ext_ref, normed_ref, out_ref, loads, sems):
    ext_copy = pltpu.make_async_copy(ext_hbm, ext_ref, loads.at[0])
    normed_copy = pltpu.make_async_copy(normed_hbm, normed_ref, loads.at[1])
    ext_copy.start()
    normed_copy.start()
    ext_copy.wait()
    normed_copy.wait()
    lags, slots, _ = out_ref.shape
    samples = normed_ref.shape[0]
    receivers = normed_ref[...]
    group = max(1, 128 // slots)
    pieces = sems.shape[0]
    piece = group * -(-lags // (group * pieces))
    copies = []
    for start in range(0, lags, group):
        stop = min(start + group, lags)
        windows = []
        for lag in range(start, stop):
            base = LANES + MAXLAG - lag
            windows.append(ext_ref[:, base : base + samples])
        left = jnp.concatenate(windows, axis=0)
        found = jnp.dot(left, receivers, preferred_element_type=jnp.float32) * scale
        out_ref[start:stop] = found.reshape(stop - start, slots, LANES)
        if stop % piece == 0 or stop == lags:
            begin = len(copies) * piece
            copy = pltpu.make_async_copy(
                out_ref.at[begin:stop], out_hbm.at[begin:stop], sems.at[len(copies)]
            )
            copy.start()
            copies.append(copy)
    for copy in copies:
        copy.wait()


def per_device(n_chan, n_tm, raw_strain, fir_taps, source_picks):
    n = n_chan * n_tm
    own = raw_strain.shape[1] // DEC
    rows = own + 8
    samples = own * n
    slots = source_picks.shape[2]
    vmem = pl.BlockSpec(memory_space=pltpu.VMEM)
    anywhere = pl.BlockSpec(memory_space=pl.ANY)
    picks = source_picks.transpose(0, 2, 1)
    traces = n_chan * slots
    sum_width = 3 * LANES + pl.cdiv(3 * traces, LANES) * LANES
    tile_width = pl.cdiv(rows // 8 * traces, LANES) * LANES
    normed, ext = pl.pallas_call(
        functools.partial(exchange_kernel, n_chan, n_tm),
        out_shape=(
            jax.ShapeDtypeStruct((samples, LANES), jnp.bfloat16),
            jax.ShapeDtypeStruct((traces, samples + 2 * LANES), jnp.bfloat16),
        ),
        in_specs=[anywhere, anywhere, anywhere],
        out_specs=(vmem, vmem),
        scratch_shapes=[
            pltpu.VMEM((n_chan, raw_strain.shape[1], n_tm * LANES), jnp.bfloat16),
            pltpu.SMEM(fir_taps.shape, jnp.float32),
            pltpu.SMEM(picks.shape, jnp.int32),
            pltpu.VMEM((n, rows, LANES), jnp.float32),
            pltpu.VMEM((n, rows, LANES), jnp.float32),
            pltpu.VMEM((samples + 2 * HALF_WIN, sum_width), jnp.bfloat16),
            pltpu.VMEM((n_chan, 3 * rows, n_tm * LANES), jnp.bfloat16),
            pltpu.VMEM((8, n_chan * traces), jnp.float32),
            pltpu.VMEM((n_chan, 8, n_chan * traces), jnp.float32),
            pltpu.VMEM((n_chan, 8, tile_width), jnp.float32),
            pltpu.VMEM((n, 8, tile_width), jnp.float32),
            pltpu.SemaphoreType.DMA((n_chan + 2,)),
            pltpu.SemaphoreType.DMA((6, n)),
        ],
        compiler_params=pltpu.CompilerParams(
            collective_id=0, has_side_effects=True, vmem_limit_bytes=60 * 2**20
        ),
    )(raw_strain, fir_taps, picks)
    out_shape = (2 * MAXLAG + 1, traces, LANES)
    return pl.pallas_call(
        functools.partial(correlate_kernel, 1.0 / math.sqrt(samples)),
        out_shape=jax.ShapeDtypeStruct(out_shape, jnp.float32),
        in_specs=[anywhere, anywhere],
        out_specs=anywhere,
        scratch_shapes=[
            pltpu.VMEM(ext.shape, ext.dtype),
            pltpu.VMEM(normed.shape, normed.dtype),
            pltpu.VMEM(out_shape, jnp.float32),
            pltpu.SemaphoreType.DMA((2,)),
            pltpu.SemaphoreType.DMA((6,)),
        ],
        compiler_params=pltpu.CompilerParams(vmem_limit_bytes=60 * 2**20),
    )(ext, normed)


def solution(mesh):
    placed = (P("tm", "chan", "groups"), P(), P(("groups", "chan"), None, None))
    return jax.shard_map(
        functools.partial(per_device, mesh.shape["chan"], mesh.shape["tm"]),
        mesh=mesh,
        in_specs=placed,
        out_specs=P(None, None, ("groups", "chan", "tm")),
        check_vma=False,
    )
```
